32 devices in a mesh: groups: 2 (over y), ctx: 4 (over z), dp: 2 (over x), head: 2 (over core).
Axes of the slice: x: 2, y: 2, z: 4, core: 2. Of those that a mesh axis runs over, the one named last changes fastest.
Arguments:
- ssm_input: bfloat16 [4, 1024, 4096], P(('groups', 'dp'), 'ctx', 'head'), parts along dimension 0, may hold values from -6 to 6
- state_maps: bfloat16 [4, 1024, 256], P(('groups', 'dp'), 'ctx'), parts along dimension 0, may hold values from -6 to 6
- gate_input: bfloat16 [4, 1024, 4096], P(('groups', 'dp'), 'ctx', 'head'), parts along dimension 0, may hold values from -6 to 6
- step_raw: float32 [4, 1024, 64], P(('groups', 'dp'), 'ctx', 'head'), parts along dimension 0, may hold values from -6 to 17
- conv_weight: float32 [4, 4096], P(None, 'head'), may hold values from -3 to 3
- conv_bias: float32 [4096], P('head'), may hold values from -1 to -0.2
- map_conv_weight: float32 [4, 256], replicated, may hold values from -3 to 3
- map_conv_bias: float32 [256], replicated, may hold values from -1 to -0.2
- step_bias: float32 [64], P('head'), may hold values from -0.3 to 0.3
- decay_log: float32 [64], P('head')
- skip_gain: float32 [64], P('head'), may hold values from 0.1 to 4
- norm_gain: float32 [4096], P('head'), may hold values from 0.25 to 1.75
- out_weight: bfloat16 [4096, 2048], P(('ctx', 'dp'), 'head'), may hold values from -0.09375 to 0.09375
Outputs:
- mixed: bfloat16 [4, 1024, 2048], P(('groups', 'dp'), 'ctx', 'head'), parts along dimension 0
The draws below stay inside these ranges and needn't reach their ends.
There are 2 independent parts, one for each index of `groups`. The reference program is written for one: setup_inputs(seed, part) draws one part's arguments, and reference() takes and returns one part's arrays. A program takes and returns all parts, laid end to end along the dimension named above; an argument that names none is the same for every part. Nothing has to cross between parts.
All inputs are finite; a program needn't handle non-finite values.
Results may differ from the reference program's by a relative error of at most 0.011.
The reference program's roundings to bfloat16 on the way count: a program that leaves them out, or rounds other values in their place, can miss the bound.
Values may be sent and summed in bfloat16 or wider, within the bound.
A program may use at most 128 MiB of HBM per device.

```python
import math
import jax
import jax.numpy as jnp
from jax import lax

D = 2048
SSD_HEADS = 64
HEAD_DIM = 64
STATE = 128
BLOCK = 256
CONV = 4
TOK_DEV = 256
E = 4096
SEQUENCE_TOKENS = 1024
BATCH_COUNT = 2


def centered_field(key, shape):
    field = jax.random.truncated_normal(key, -6.0, 6.0, shape, jnp.float32)
    return field.astype(jnp.bfloat16)


def draw_ssm_input(key, part):
    return centered_field(jax.random.fold_in(key, 11), (BATCH_COUNT, SEQUENCE_TOKENS, E))


def draw_state_maps(key, part):
    return centered_field(jax.random.fold_in(key, 23), (BATCH_COUNT, SEQUENCE_TOKENS, 2 * STATE))


def draw_step_raw(key, part):
    random_subkeys = jax.random.split(key, 4)
    blocks = SEQUENCE_TOKENS // TOK_DEV
    level_low = math.log(0.01)
    dt_level = jnp.exp(jax.random.uniform(random_subkeys[0], (BATCH_COUNT, blocks, 1, SSD_HEADS), jnp.float32, level_low, math.log(0.03)))
    dt_level = jnp.broadcast_to(dt_level, (BATCH_COUNT, blocks, TOK_DEV, SSD_HEADS)).reshape(BATCH_COUNT, SEQUENCE_TOKENS, SSD_HEADS)
    dt_noise = jnp.exp(jax.random.uniform(random_subkeys[1], (BATCH_COUNT, SEQUENCE_TOKENS, SSD_HEADS), jnp.float32, -0.35, 0.35))
    target_step_size = dt_level * dt_noise
    spike_positions = jax.random.randint(random_subkeys[2], (BATCH_COUNT, 1, 3), 0, SEQUENCE_TOKENS)
    spike_mask = jnp.any(jnp.arange(SEQUENCE_TOKENS)[None, :, None] == spike_positions, axis=-1)
    spike_length = jax.random.uniform(random_subkeys[3], (BATCH_COUNT, SEQUENCE_TOKENS, SSD_HEADS), jnp.float32, 8.0, 16.0)
    target_step_size = jnp.where(spike_mask[:, :, None], spike_length, target_step_size)
    return jnp.log(jnp.expm1(target_step_size))


def draw_decay_log(key, part):
    random_subkeys = jax.random.split(key, 3)
    slow_share = 0.5
    chooser = jax.random.uniform(random_subkeys[0], (SSD_HEADS,), jnp.float32)
    slow_rate = jax.random.uniform(random_subkeys[1], (SSD_HEADS,), jnp.float32, 0.8, 1.6) / (0.02 * SEQUENCE_TOKENS)
    fast_rate = jnp.exp(jax.random.uniform(random_subkeys[2], (SSD_HEADS,), jnp.float32, math.log(0.8), math.log(2.5)))
    return jnp.log(jnp.where(chooser < slow_share, slow_rate, fast_rate))


def level_of(key, shape, cuts, smallest, largest):
    factor_of, own = 1.0, jax.random.fold_in(key, 6)
    for axis_at, blocks in cuts:
        steps = jnp.exp(jax.random.uniform(jax.random.fold_in(own, axis_at), (blocks,), jnp.float32, smallest / len(cuts), largest / len(cuts)))
        factor_of = factor_of * jnp.repeat(steps, shape[axis_at] // blocks).reshape([-1 if axis == axis_at else 1 for axis in range(len(shape))])
    return factor_of


def normal_values(own_key, dims, width, limit, cuts=(), held_as=jnp.bfloat16):
    factor_of = level_of(own_key, dims, cuts, -0.22, 0.18) if cuts else 1.0
    values = jax.random.normal(own_key, dims, jnp.float32) * width * factor_of
    return jnp.minimum(jnp.maximum(values, -limit), limit).astype(held_as)


def setup_inputs(seed: int = 0, part: int = 0) -> dict:
    splits = jax.random.split(jax.random.key(seed), 14)
    own_keys = jax.random.split(jax.random.fold_in(splits[13], part), 14)
    return {
        "ssm_input": draw_ssm_input(jax.random.fold_in(jax.random.fold_in(splits[13], part), 71), part),
        "state_maps": draw_state_maps(jax.random.fold_in(jax.random.fold_in(splits[13], part), 71), part),
        "gate_input": normal_values(own_keys[2], (BATCH_COUNT, SEQUENCE_TOKENS, E), 1.0, 6.0, ((0, 2), (1, 4), (2, 2))),
        "step_raw": draw_step_raw(jax.random.fold_in(jax.random.fold_in(splits[13], part), 71), part),
        "conv_weight": normal_values(splits[4], (CONV, E), CONV ** -0.5, 3.0, ((1, 2),), jnp.float32),
        "conv_bias": jnp.clip(-1.0 + 0.8 * jax.random.uniform(splits[5], (E,), jnp.float32) ** level_of(splits[5], (E,), ((0, 2),), -0.2, 0.2), -1.0, -0.2),
        "map_conv_weight": normal_values(splits[6], (CONV, 2 * STATE), CONV ** -0.5, 3.0, (), jnp.float32),
        "map_conv_bias": jnp.clip(jax.random.uniform(splits[7], (2 * STATE,), jnp.float32, -1.0, -0.2), -1.0, -0.2),
        "step_bias": jnp.clip(jax.random.uniform(splits[8], (SSD_HEADS,), jnp.float32, -0.3, 0.3) * level_of(splits[8], (SSD_HEADS,), ((0, 2),), -0.4, 0.0), -0.3, 0.3),
        "decay_log": draw_decay_log(jax.random.fold_in(splits[13], 71), part),
        "skip_gain": jnp.clip(jnp.exp(math.log(4.0) - 3.6888794 * jax.random.uniform(splits[10], (SSD_HEADS,), jnp.float32) ** level_of(splits[10], (SSD_HEADS,), ((0, 2),), -0.2, 0.2)), 0.1, 4.0),
        "norm_gain": jnp.clip(1.0 + 0.15 * jax.random.normal(splits[11], (E,), jnp.float32), 0.25, 1.75),
        "out_weight": normal_values(splits[12], (E, D), E ** -0.5, 0.09375, ((0, 8), (1, 2))),
    }


def causal_conv(signal, taps, bias):
    conv_width = taps.shape[0]
    token_count = signal.shape[1]
    padded = jnp.pad(signal.astype(jnp.float32), ((0, 0), (conv_width - 1, 0), (0, 0)))
    summed = jnp.zeros(signal.shape, jnp.float32) + bias[None, None, :]
    for offset in range(conv_width):
        summed = summed + taps[offset][None, None, :] * padded[:, offset:offset + token_count, :]
    return jax.nn.silu(summed).astype(jnp.bfloat16)

def reference(ssm_input, state_maps, gate_input, step_raw, conv_weight, conv_bias, map_conv_weight, map_conv_bias, step_bias, decay_log, skip_gain, norm_gain, out_weight):
    values = causal_conv(ssm_input, conv_weight, conv_bias)
    maps_out = causal_conv(state_maps, map_conv_weight, map_conv_bias)
    in_maps = maps_out[..., :STATE]
    out_maps = maps_out[..., STATE:]
    step_size = jax.nn.softplus(step_raw + step_bias)
    log_step = step_size * -jnp.exp(decay_log)
    head_count = decay_log.shape[0]
    block_count = SEQUENCE_TOKENS // BLOCK
    positions = jnp.arange(BLOCK)
    causal_mask = positions[:, None] >= positions[None, :]

    def block_step(carry_state, pieces):
        block_values, block_in, block_out, block_step_size, block_log = pieces
        cumulative = jnp.cumsum(block_log, axis=0)
        scores = jnp.dot(block_out, block_in.T, preferred_element_type=jnp.float32)
        log_gap = jnp.where(causal_mask[None, :, :], cumulative.T[:, :, None] - cumulative.T[:, None, :], -jnp.inf)
        mix_weights = (scores[None, :, :] * jnp.exp(log_gap) * block_step_size.T[:, None, :]).astype(jnp.bfloat16)
        diagonal_part = jnp.einsum('hts,shp->thp', mix_weights.astype(jnp.float32), block_values.astype(jnp.float32))
        tail_decay = jnp.exp(cumulative[-1][None, :] - cumulative) * block_step_size
        weighted_maps = (block_in.astype(jnp.float32)[:, None, :] * tail_decay[:, :, None]).astype(jnp.bfloat16)
        block_state = jnp.einsum('shp,shn->hpn', block_values.astype(jnp.float32), weighted_maps.astype(jnp.float32))
        held_state = carry_state.astype(jnp.bfloat16)
        carried = jnp.exp(cumulative)[:, :, None] * jnp.einsum('tn,hpn->thp', block_out.astype(jnp.float32), held_state.astype(jnp.float32))
        outputs = diagonal_part + carried + skip_gain[None, :, None] * block_values.astype(jnp.float32)
        next_state = jnp.exp(cumulative[-1])[:, None, None] * carry_state + block_state
        return (next_state, outputs)

    def per_sequence(sequence_pieces):
        seq_values, seq_in, seq_out, seq_step, seq_log = sequence_pieces
        pieces = (seq_values.reshape(block_count, BLOCK, head_count, HEAD_DIM), seq_in.reshape(block_count, BLOCK, STATE), seq_out.reshape(block_count, BLOCK, STATE), seq_step.reshape(block_count, BLOCK, head_count), seq_log.reshape(block_count, BLOCK, head_count))
        start_state = jnp.zeros((head_count, HEAD_DIM, STATE), jnp.float32)
        final_state, outputs = lax.scan(block_step, start_state, pieces)
        return outputs.reshape(SEQUENCE_TOKENS, head_count * HEAD_DIM)
    ssm_out = lax.map(per_sequence, (values, in_maps, out_maps, step_size, log_step))
    gated_values = ssm_out * jax.nn.silu(gate_input.astype(jnp.float32))
    normed = (gated_values * lax.rsqrt(lax.optimization_barrier(jnp.mean(gated_values * gated_values, axis=-1, keepdims=True)) + 1e-05) * norm_gain).astype(jnp.bfloat16)
    flat_rows = normed.reshape(-1, normed.shape[-1])
    mixed_out = jnp.dot(flat_rows, out_weight, preferred_element_type=jnp.float32)
    return mixed_out.reshape(BATCH_COUNT, SEQUENCE_TOKENS, out_weight.shape[1]).astype(jnp.bfloat16)
```

```python
import functools

import jax
import jax.numpy as jnp
from jax import lax
from jax.experimental import pallas as pl
from jax.experimental.pallas import tpu as pltpu
from jax.sharding import PartitionSpec as P

MESH = pl.DeviceIdType.MESH
F32, BF16 = jnp.float32, jnp.bfloat16
EDGE = 16
CHUNK = 512


def silu(v):
    return 0.5 * v * (1.0 + jnp.tanh(0.5 * v))


def dot(a, b):
    return jnp.dot(a, b, preferred_element_type=F32)


def kernel(
    sizes,
    ssm, maps, gate, step_raw, taps, bias, map_taps, map_bias, step_bias, decay, skip, gain, w_in,
    out,
    wfull, normed, states, held, handed, y_ref, xs_ref, col, cum_t, tail_t, step_t, scores, b_t, c_map,
    edge_x, edge_m, pad, pad_m, cum_buf, square, square_peer,
    w_sem, edge_send, edge_recv, zup_sem, zdn_sem, z_recv, x_send, x_recv, y_send, y_recv,
    st_send, st_recv, n_send, n_recv, q_sem,
):
    nc, nd, ng = sizes
    tok, channels = ssm.shape
    heads = step_raw.shape[1]
    rows = w_in.shape[0]
    part = max(16, (rows * 3 // 8) // 16 * 16)
    mine = rows - part
    chunks = channels // CHUNK
    pairs = CHUNK // 128
    g, c = lax.axis_index("groups"), lax.axis_index("ctx")
    d, h = lax.axis_index("dp"), lax.axis_index("head")
    half = tok // 2

    def span(start, size):
        return pl.ds(pl.multiple_of(start, 16), size)

    def slab(cc, dd):
        return cc * nd + dd

    def mine_of(cc, dd):
        return wfull.at[span(slab(cc, dd) * rows + g * part, mine)]

    def copy(src, dst, send, recv, target):
        return pltpu.make_async_remote_copy(
            src_ref=src, dst_ref=dst, send_sem=send, recv_sem=recv,
            device_id=target, device_id_type=MESH,
        )

    def z_up(s):
        return copy(mine_of(s, d), mine_of(s, d), zup_sem.at[s], z_recv.at[s], {"ctx": c + 1})

    def z_dn(s):
        return copy(mine_of(s, d), mine_of(s, d), zdn_sem.at[s], z_recv.at[s], {"ctx": c - 1})

    def x_out(s, peer):
        return copy(mine_of(s, d), mine_of(s, d), x_send.at[slab(s, peer)], x_recv.at[slab(s, d)], {"dp": peer})

    def x_in(s, peer):
        return copy(mine_of(s, peer), mine_of(s, peer), x_send.at[slab(s, peer)], x_recv.at[slab(s, peer)], {"dp": peer})

    def y_out(b):
        ref = wfull.at[span(b * rows + g * mine, part)]
        return copy(ref, ref, y_send.at[b], y_recv.at[b], {"groups": 1 - g})

    def y_in(b):
        ref = wfull.at[span(b * rows + (1 - g) * mine, part)]
        return copy(ref, ref, y_send.at[b], y_recv.at[b], {"groups": 1 - g})

    def others(do):
        def one(o, _):
            do(lax.rem(d + o, nd))
            return 0
        lax.fori_loop(1, nd, one, 0)

    own = slab(c, d)
    load = pltpu.make_async_copy(w_in, wfull.at[span(own * rows, rows)], w_sem)
    load.start()

    barrier = pltpu.get_barrier_semaphore()

    def greet(target):
        pl.semaphore_signal(barrier, inc=1, device_id=target, device_id_type=MESH)

    @pl.when(c > 0)
    def _():
        greet({"ctx": c - 1})

    @pl.when(c + 1 < nc)
    def _():
        greet({"ctx": c + 1})

    others(lambda peer: greet({"dp": peer}))
    greet({"groups": 1 - g})
    greet({"head": 1 - h})
    load.wait()
    pl.semaphore_wait(barrier, nd + 1 + jnp.where(c > 0, 1, 0) + jnp.where(c + 1 < nc, 1, 0))

    def edges():
        return (
            copy(ssm.at[pl.ds(tok - EDGE, EDGE)], edge_x, edge_send.at[0], edge_recv.at[0], {"ctx": c + 1}),
            copy(maps.at[pl.ds(tok - EDGE, EDGE)], edge_m, edge_send.at[1], edge_recv.at[1], {"ctx": c + 1}),
        )

    @pl.when(c + 1 < nc)
    def _():
        for one in edges():
            one.start()
        z_up(c).start()

    @pl.when(c > 0)
    def _():
        z_dn(c).start()

    others(lambda peer: x_out(c, peer).start())

    raw = step_raw[...] + step_bias[...]
    step = jnp.maximum(raw, 0.0) + jnp.log1p(jnp.exp(-jnp.abs(raw)))
    cum_buf[...] = jnp.zeros_like(cum_buf)
    cum_buf[half : half + tok, :heads] = step
    step_t[...] = jnp.transpose(cum_buf[half : half + tok, :])[: step_t.shape[0]]
    cum_buf[half : half + tok, :heads] = step * -jnp.exp(decay[...])
    by = 1
    while by < tok:
        cum_buf[half : half + tok, :] = cum_buf[half : half + tok, :] + cum_buf[half - by : half - by + tok, :]
        by *= 2
    cum = cum_buf[half : half + tok, :]
    cum_t[...] = jnp.transpose(cum)[: cum_t.shape[0]]
    tail_t[...] = jnp.exp(cum_t[:, tok - 1 : tok] - cum_t[...]) * step_t[...]
    for i in range(heads):
        col[i] = jnp.broadcast_to(cum[:, i : i + 1], (tok, 128))

    @pl.when(c == 0)
    def _():
        edge_x[...] = jnp.zeros_like(edge_x)
        edge_m[...] = jnp.zeros_like(edge_m)
        held[...] = jnp.zeros_like(held)

    @pl.when(c > 0)
    def _():
        for one in edges():
            one.wait_recv()

    low = lax.broadcasted_iota(jnp.int32, (1, 128), 1) < channels // heads

    pad_m[0:8] = edge_m[...].astype(F32)[EDGE - 8 :]
    pad_m[8 : 8 + tok] = maps[...].astype(F32)
    total = jnp.broadcast_to(map_bias[...], (tok, maps.shape[1]))
    for k in range(4):
        total = total + map_taps[k : k + 1, :] * pad_m[5 + k : 5 + k + tok]
    both = silu(total).astype(BF16)
    n_state = maps.shape[1] // 2
    c_map[...] = both[:, n_state:]
    b_t[...] = jnp.transpose(both[:, :n_state].astype(F32))
    scores[...] = dot(c_map[...], b_t[...].astype(BF16))

    def lanes_of(j):
        return pl.ds(pl.multiple_of(j * 128, 128), 128)

    def first(j, _):
        lanes = lanes_of(j)
        pad[0:8] = edge_x[:, lanes].astype(F32)[EDGE - 8 :]
        pad[8 : 8 + tok] = ssm[:, lanes].astype(F32)
        total = jnp.broadcast_to(bias[:, lanes], (tok, 128))
        for k in range(4):
            total = total + taps[k : k + 1, lanes] * pad[5 + k : 5 + k + tok]
        xs = silu(total).astype(BF16)
        xs_ref[:, lanes] = xs
        parts = []
        for i in range(2):
            weighted = (b_t[...] * tail_t[pl.ds(2 * j + i, 1), :]).astype(BF16)
            parts.append(dot(weighted, xs))
        states[:, lanes] = jnp.where(low, parts[0], parts[1])
        return 0

    lax.fori_loop(0, channels // 128, first, 0)

    def st_copy(q):
        return copy(handed.at[q], held.at[q], st_send.at[q], st_recv.at[q], {"ctx": c + 1})

    def chain(q):
        @pl.when(c > 0)
        def _():
            st_copy(q).wait_recv()

        @pl.when(c + 1 < nc)
        def _():
            for p in range(pairs):
                j = q * pairs + p
                decayed = jnp.where(low, col[2 * j, tok - 1 : tok, :], col[2 * j + 1, tok - 1 : tok, :])
                piece = slice(p * 128, p * 128 + 128)
                following = jnp.exp(decayed) * held[q, :, piece].astype(F32) + states[:, j * 128 : j * 128 + 128]
                handed[q, :, piece] = following.astype(BF16)
            st_copy(q).start()

    rows_i = lax.broadcasted_iota(jnp.int32, (half, half), 0)
    cols_i = lax.broadcasted_iota(jnp.int32, (half, half), 1)
    causal = rows_i >= cols_i

    def diag(j, _):
        lanes = lanes_of(j)
        xs = xs_ref[:, lanes]
        tops, bottoms = [], []
        for i in range(2):
            at = 2 * j + i
            row = cum_t[pl.ds(at, 1), :]
            sized = step_t[pl.ds(at, 1), :]
            column = col[at]
            upper, lower = column[:half], column[half:]
            q00 = scores[:half, :half] * jnp.exp(jnp.where(causal, upper - row[:, :half], -jnp.inf)) * sized[:, :half]
            q10 = scores[half:, :half] * jnp.exp(lower - row[:, :half]) * sized[:, :half]
            q11 = scores[half:, half:] * jnp.exp(jnp.where(causal, lower - row[:, half:], -jnp.inf)) * sized[:, half:]
            tops.append(dot(q00.astype(BF16), xs[:half]))
            bottoms.append(dot(q10.astype(BF16), xs[:half]) + dot(q11.astype(BF16), xs[half:]))
        skips = jnp.where(low, skip[2 * j], skip[2 * j + 1])
        y_ref[:half, lanes] = jnp.where(low, tops[0], tops[1]) + skips * xs[:half].astype(F32)
        y_ref[half:, lanes] = jnp.where(low, bottoms[0], bottoms[1]) + skips * xs[half:].astype(F32)
        return 0

    def z_step(k):
        below, above = c - k, c + k

        @pl.when(below >= 0)
        def _():
            z_up(below).wait_recv()

            @pl.when(c + 1 < nc)
            def _():
                z_up(below).start()

            others(lambda peer: x_out(below, peer).start())
            y_out(slab(below, d)).start()

        @pl.when(above < nc)
        def _():
            z_dn(above).wait_recv()

            @pl.when(c > 0)
            def _():
                z_dn(above).start()

            others(lambda peer: x_out(above, peer).start())
            y_out(slab(above, d)).start()

    def x_step(k):
        for s, valid in ([(c, c >= 0)] if k == 0 else [(c - k, c - k >= 0), (c + k, c + k < nc)]):
            @pl.when(valid)
            def _(s=s):
                def one(peer):
                    x_in(s, peer).wait_recv()
                    y_out(slab(s, peer)).start()
                others(one)

    chain(0)
    lax.fori_loop(0, channels // 128, diag, 0)
    for q in range(1, chunks):
        chain(q)
        if q == 1:
            z_step(1)
            x_step(0)

    square[...] = jnp.zeros_like(square)

    def n_copy(q):
        ref = normed.at[h * chunks + q]
        return copy(ref, ref, n_send.at[q], n_recv.at[q], {"head": 1 - h})

    def n_in(q):
        ref = normed.at[(1 - h) * chunks + q]
        return copy(ref, ref, n_send.at[q], n_recv.at[q], {"head": 1 - h})

    for q in range(chunks):
        for p in range(pairs):
            j = q * pairs + p
            lanes = slice(j * 128, j * 128 + 128)
            piece = slice(p * 128, p * 128 + 128)
            carried = dot(c_map[...], held[q, :, piece])
            grown = jnp.exp(jnp.where(low, col[2 * j], col[2 * j + 1]))
            v = (y_ref[:, lanes] + carried * grown) * silu(gate[:, lanes].astype(F32))
            square[...] += v * v
            normed[h * chunks + q, :, piece] = (v * gain[:, lanes]).astype(BF16)
        n_copy(q).start()

    def q_copy():
        return copy(square, square_peer, q_sem.at[0], q_sem.at[1], {"head": 1 - h})

    q_copy().start()

    for k in range(2, nc):
        z_step(k)
        x_step(k - 1)
    x_step(nc - 1)

    for q in range(chunks):
        n_in(q).wait_recv()
    q_copy().wait_recv()

    def arrived(b, _):
        @pl.when(b != own)
        def _():
            y_in(b).wait_recv()
        return 0

    lax.fori_loop(0, nc * nd, arrived, 0)

    sums = jnp.sum(square[...] + square_peer[...], axis=1, keepdims=True)
    scale = lax.rsqrt(sums / (2 * channels) + 1e-05)

    width = 256

    def project(n, _):
        at = pl.ds(pl.multiple_of(n * width, width), width)
        acc = jnp.zeros((tok, width), F32)
        for q in range(2 * chunks):
            acc = acc + dot(normed[q], wfull[q * CHUNK : (q + 1) * CHUNK, at])
        out[:, at] = (acc * scale).astype(BF16)
        return 0

    lax.fori_loop(0, out.shape[1] // width, project, 0)

    def sent_x(s, _):
        others(lambda peer: x_out(s, peer).wait_send())
        return 0

    lax.fori_loop(0, nc, sent_x, 0)

    def sent_y(b, _):
        @pl.when(b != own)
        def _():
            y_out(b).wait_send()
        return 0

    lax.fori_loop(0, nc * nd, sent_y, 0)

    @pl.when(c + 1 < nc)
    def _():
        for one in edges():
            one.wait_send()
        for q in range(chunks):
            st_copy(q).wait_send()

        def sent(s, _):
            z_up(s).wait_send()
            return 0
        lax.fori_loop(0, c + 1, sent, 0)

    @pl.when(c > 0)
    def _():
        def sent(s, _):
            z_dn(s).wait_send()
            return 0
        lax.fori_loop(c, nc, sent, 0)

    for q in range(chunks):
        n_copy(q).wait_send()
    q_copy().wait_send()


def on_device(sizes, ssm, maps, gate, step_raw, taps, bias, map_taps, map_bias, step_bias, decay, skip, gain, w):
    nc, nd, ng = sizes
    tok, channels = ssm.shape[1:]
    heads = step_raw.shape[2]
    n_state = maps.shape[2] // 2
    features = w.shape[1]
    chunks = channels // CHUNK
    slabs = nc * nd
    dma = pltpu.SemaphoreType.DMA
    vmem = pl.BlockSpec(memory_space=pltpu.VMEM)
    result = pl.pallas_call(
        functools.partial(kernel, sizes),
        out_shape=jax.ShapeDtypeStruct((tok, features), BF16),
        in_specs=[vmem] * 10 + [pl.BlockSpec(memory_space=pltpu.SMEM), vmem, pl.BlockSpec(memory_space=pl.ANY)],
        out_specs=vmem,
        scratch_shapes=[
            pltpu.VMEM((slabs * w.shape[0], features), BF16),
            pltpu.VMEM((2 * chunks, tok, CHUNK), BF16),
            pltpu.VMEM((n_state, channels), F32),
            pltpu.VMEM((chunks, n_state, CHUNK), BF16),
            pltpu.VMEM((chunks, n_state, CHUNK), BF16),
            pltpu.VMEM((tok, channels), F32),
            pltpu.VMEM((tok, channels), BF16),
            pltpu.VMEM((heads, tok, 128), F32),
            pltpu.VMEM((heads, tok), F32),
            pltpu.VMEM((heads, tok), F32),
            pltpu.VMEM((heads, tok), F32),
            pltpu.VMEM((tok, tok), F32),
            pltpu.VMEM((n_state, tok), F32),
            pltpu.VMEM((tok, n_state), BF16),
            pltpu.VMEM((EDGE, channels), BF16),
            pltpu.VMEM((EDGE, 2 * n_state), BF16),
            pltpu.VMEM((tok + 8, 128), F32),
            pltpu.VMEM((tok + 8, 2 * n_state), F32),
            pltpu.VMEM((tok + tok // 2, 128), F32),
            pltpu.VMEM((tok, 128), F32),
            pltpu.VMEM((tok, 128), F32),
            dma, dma((2,)), dma((2,)), dma((nc,)), dma((nc,)), dma((nc,)),
            dma((slabs,)), dma((slabs,)), dma((slabs,)), dma((slabs,)),
            dma((chunks,)), dma((chunks,)), dma((chunks,)), dma((chunks,)), dma((2,)),
        ],
        compiler_params=pltpu.CompilerParams(
            collective_id=0, has_side_effects=True, vmem_limit_bytes=48 * 1024 * 1024
        ),
    )(
        ssm[0], maps[0], gate[0], step_raw[0], taps, bias[None], map_taps, map_bias[None],
        step_bias[None], decay[None], skip, gain[None], w,
    )
    return result[None]


def solution(mesh):
    sizes = (mesh.shape["ctx"], mesh.shape["dp"], mesh.shape["groups"])
    placed = (
        P(("groups", "dp"), "ctx", "head"),
        P(("groups", "dp"), "ctx", None),
        P(("groups", "dp"), "ctx", "head"),
        P(("groups", "dp"), "ctx", "head"),
        P(None, "head"),
        P("head"),
        P(),
        P(),
        P("head"),
        P("head"),
        P("head"),
        P("head"),
        P(("ctx", "dp"), "head"),
    )
    return jax.shard_map(
        functools.partial(on_device, sizes),
        mesh=mesh,
        in_specs=placed,
        out_specs=P(("groups", "dp"), "ctx", "head"),
        check_vma=False,
    )
```

```python
import functools

import jax
import jax.numpy as jnp
from jax import lax
from jax.experimental import pallas as pl
from jax.experimental.pallas import tpu as pltpu
from jax.sharding import PartitionSpec as P

MESH = pl.DeviceIdType.MESH
F32, BF16 = jnp.float32, jnp.bfloat16
EDGE = 16
CHUNK = 512
PIECES = 2


def silu(v):
    return 0.5 * v * (1.0 + jnp.tanh(0.5 * v))


def dot(a, b):
    return jnp.dot(a, b, preferred_element_type=F32)


def kernel(
    sizes, split,
    *refs,
):
    n_in_refs = 13
    hbm = refs[:n_in_refs]
    out = refs[n_in_refs]
    local = refs[n_in_refs + 1 : 2 * n_in_refs]
    (
        wfull, normed, states, held, handed, y_ref, xs_ref, col, cum_t, tail_t, step_t, scores, b_t, c_map,
        edge_x, edge_m, pad, pad_m, cum_buf, square, square_peer, skip_col, stage, acc_ref, p_out, p_in,
        in_sem, w_sem, edge_send, edge_recv, zup_sem, zdn_sem, z_recv, x_send, x_recv, y_send, y_recv,
        st_send, st_recv, n_send, n_recv, q_sem, r_send, r_recv, f_send, f_recv, p_send, p_recv,
    ) = refs[2 * n_in_refs :]
    w_in = hbm[-1]
    ssm, maps, gate, step_raw, taps, bias, map_taps, map_bias, step_bias, decay, skip, gain = local
    nc, nd, ng = sizes
    tok, channels = ssm.shape
    heads = step_raw.shape[0]
    rows = w_in.shape[0]
    features = w_in.shape[1]
    pieces, piece_width, _ = wfull.shape[0], wfull.shape[2], 0
    part = rows // 2 if split else max(16, (rows * 3 // 8) // 16 * 16)
    mine = rows - part
    chunks = channels // CHUNK
    pairs = CHUNK // 128
    g, c = lax.axis_index("groups"), lax.axis_index("ctx")
    d, h = lax.axis_index("dp"), lax.axis_index("head")
    half = tok // 2

    def span(start, size):
        return pl.ds(pl.multiple_of(start, 16), size)

    def slab(cc, dd):
        return cc if split else cc * nd + dd

    slabs = nc if split else nc * nd

    def mine_of(cc, dd, n):
        return wfull.at[n, span(slab(cc, dd) * rows + g * part, mine)]

    def copy(src, dst, send, recv, target):
        return pltpu.make_async_remote_copy(
            src_ref=src, dst_ref=dst, send_sem=send, recv_sem=recv,
            device_id=target, device_id_type=MESH,
        )

    def z_up(s, n):
        ref, at = mine_of(s, d, n), n * nc + s
        return copy(ref, ref, zup_sem.at[at], z_recv.at[at], {"ctx": c + 1})

    def z_dn(s, n):
        ref, at = mine_of(s, d, n), n * nc + s
        return copy(ref, ref, zdn_sem.at[at], z_recv.at[at], {"ctx": c - 1})

    def x_out(s, peer):
        ref = mine_of(s, d, 0)
        return copy(ref, ref, x_send.at[slab(s, peer)], x_recv.at[slab(s, d)], {"dp": peer})

    def x_in(s, peer):
        ref = mine_of(s, peer, 0)
        return copy(ref, ref, x_send.at[slab(s, peer)], x_recv.at[slab(s, peer)], {"dp": peer})

    def y_out(b, n):
        ref, at = wfull.at[n, span(b * rows + g * mine, part)], n * slabs + b
        return copy(ref, ref, y_send.at[at], y_recv.at[at], {"groups": 1 - g})

    def y_in(b, n):
        ref, at = wfull.at[n, span(b * rows + (1 - g) * mine, part)], n * slabs + b
        return copy(ref, ref, y_send.at[at], y_recv.at[at], {"groups": 1 - g})

    def others(do):
        def one(o, _):
            do(lax.rem(d + o, nd))
            return 0
        lax.fori_loop(1, nd, one, 0)

    own = slab(c, d)
    loads = [
        pltpu.make_async_copy(
            w_in.at[:, n * piece_width : (n + 1) * piece_width], wfull.at[n, span(own * rows, rows)], w_sem.at[n]
        )
        for n in range(pieces)
    ]
    fetches = [pltpu.make_async_copy(a, b, in_sem.at[i]) for i, (a, b) in enumerate(zip(hbm[:-1], local))]
    for one in loads + fetches:
        one.start()

    barrier = pltpu.get_barrier_semaphore()

    def greet(target):
        pl.semaphore_signal(barrier, inc=1, device_id=target, device_id_type=MESH)

    @pl.when(c > 0)
    def _():
        greet({"ctx": c - 1})

    @pl.when(c + 1 < nc)
    def _():
        greet({"ctx": c + 1})

    others(lambda peer: greet({"dp": peer}))
    greet({"groups": 1 - g})
    greet({"head": 1 - h})
    for one in loads + fetches[:2]:
        one.wait()
    pl.semaphore_wait(barrier, nd + 1 + jnp.where(c > 0, 1, 0) + jnp.where(c + 1 < nc, 1, 0))

    def edges():
        return (
            copy(ssm.at[pl.ds(tok - EDGE, EDGE)], edge_x, edge_send.at[0], edge_recv.at[0], {"ctx": c + 1}),
            copy(maps.at[pl.ds(tok - EDGE, EDGE)], edge_m, edge_send.at[1], edge_recv.at[1], {"ctx": c + 1}),
        )

    @pl.when(c + 1 < nc)
    def _():
        for one in edges():
            one.start()
        for n in range(pieces):
            z_up(c, n).start()

    @pl.when(c > 0)
    def _():
        for n in range(pieces):
            z_dn(c, n).start()

    if not split:
        others(lambda peer: x_out(c, peer).start())

    for one in fetches[2:]:
        one.wait()

    cum_buf[...] = jnp.zeros_like(cum_buf)
    cum_buf[:heads, :] = step_raw[:, :half]
    cum_buf[half : half + heads, :] = step_raw[:, half:]
    raw_top = jnp.transpose(cum_buf[:half, :])
    raw_bottom = jnp.transpose(cum_buf[half : tok, :])
    raw = jnp.concatenate([raw_top, raw_bottom], axis=0)[:, :heads] + step_bias[...]
    step = jnp.maximum(raw, 0.0) + jnp.log1p(jnp.exp(-jnp.abs(raw)))
    cum_buf[...] = jnp.zeros_like(cum_buf)
    cum_buf[half : half + tok, :heads] = step
    step_t[...] = jnp.transpose(cum_buf[half : half + tok, :])[: step_t.shape[0]]
    cum_buf[half : half + tok, :heads] = step * -jnp.exp(decay[...])
    by = 1
    while by < tok:
        cum_buf[half : half + tok, :] = cum_buf[half : half + tok, :] + cum_buf[half - by : half - by + tok, :]
        by *= 2
    cum = cum_buf[half : half + tok, :]
    cum_t[...] = jnp.transpose(cum)[: cum_t.shape[0]]
    tail_t[...] = jnp.exp(cum_t[:, tok - 1 : tok] - cum_t[...]) * step_t[...]
    for i in range(heads):
        col[i] = jnp.broadcast_to(cum[:, i : i + 1], (tok, 128))
        skip_col[i] = jnp.broadcast_to(skip[:, i : i + 1], (8, 128))

    @pl.when(c == 0)
    def _():
        edge_x[...] = jnp.zeros_like(edge_x)
        edge_m[...] = jnp.zeros_like(edge_m)
        held[...] = jnp.zeros_like(held)

    @pl.when(c > 0)
    def _():
        for one in edges():
            one.wait_recv()

    low = lax.broadcasted_iota(jnp.int32, (1, 128), 1) < channels // heads

    pad_m[0:8] = edge_m[...].astype(F32)[EDGE - 8 :]
    pad_m[8 : 8 + tok] = maps[...].astype(F32)
    total = jnp.broadcast_to(map_bias[...], (tok, maps.shape[1]))
    for k in range(4):
        total = total + map_taps[k : k + 1, :] * pad_m[5 + k : 5 + k + tok]
    both = silu(total).astype(BF16)
    n_state = maps.shape[1] // 2
    c_map[...] = both[:, n_state:]
    b_t[...] = jnp.transpose(both[:, :n_state].astype(F32))
    scores[...] = dot(c_map[...], b_t[...].astype(BF16))

    def lanes_of(j):
        return pl.ds(pl.multiple_of(j * 128, 128), 128)

    def first(j, _):
        lanes = lanes_of(j)
        pad[0:8] = edge_x[:, lanes].astype(F32)[EDGE - 8 :]
        pad[8 : 8 + tok] = ssm[:, lanes].astype(F32)
        total = jnp.broadcast_to(bias[:, lanes], (tok, 128))
        for k in range(4):
            total = total + taps[k : k + 1, lanes] * pad[5 + k : 5 + k + tok]
        xs = silu(total).astype(BF16)
        xs_ref[:, lanes] = xs
        parts = []
        for i in range(2):
            weighted = (b_t[...] * tail_t[pl.ds(2 * j + i, 1), :]).astype(BF16)
            parts.append(dot(weighted, xs))
        states[:, lanes] = jnp.where(low, parts[0], parts[1])
        return 0

    lax.fori_loop(0, channels // 128, first, 0)

    def st_copy(q):
        return copy(handed.at[q], held.at[q], st_send.at[q], st_recv.at[q], {"ctx": c + 1})

    def chain(q):
        @pl.when(c > 0)
        def _():
            st_copy(q).wait_recv()

        @pl.when(c + 1 < nc)
        def _():
            for p in range(pairs):
                j = q * pairs + p
                decayed = jnp.where(low, col[2 * j, tok - 1 : tok, :], col[2 * j + 1, tok - 1 : tok, :])
                piece = slice(p * 128, p * 128 + 128)
                following = jnp.exp(decayed) * held[q, :, piece].astype(F32) + states[:, j * 128 : j * 128 + 128]
                handed[q, :, piece] = following.astype(BF16)
            st_copy(q).start()

    rows_i = lax.broadcasted_iota(jnp.int32, (half, half), 0)
    cols_i = lax.broadcasted_iota(jnp.int32, (half, half), 1)
    causal = rows_i >= cols_i

    def diag(j, _):
        lanes = lanes_of(j)
        xs = xs_ref[:, lanes]
        tops, bottoms = [], []
        for i in range(2):
            at = 2 * j + i
            row = cum_t[pl.ds(at, 1), :]
            sized = step_t[pl.ds(at, 1), :]
            column = col[at]
            upper, lower = column[:half], column[half:]
            q00 = scores[:half, :half] * jnp.exp(jnp.where(causal, upper - row[:, :half], -jnp.inf)) * sized[:, :half]
            q10 = scores[half:, :half] * jnp.exp(lower - row[:, :half]) * sized[:, :half]
            q11 = scores[half:, half:] * jnp.exp(jnp.where(causal, lower - row[:, half:], -jnp.inf)) * sized[:, half:]
            tops.append(dot(q00.astype(BF16), xs[:half]))
            bottoms.append(dot(q10.astype(BF16), xs[:half]) + dot(q11.astype(BF16), xs[half:]))
        skips = jnp.where(low, skip_col[2 * j, 0:1, :], skip_col[2 * j + 1, 0:1, :])
        y_ref[:half, lanes] = jnp.where(low, tops[0], tops[1]) + skips * xs[:half].astype(F32)
        y_ref[half:, lanes] = jnp.where(low, bottoms[0], bottoms[1]) + skips * xs[half:].astype(F32)
        return 0

    def z_step(k, n):
        below, above = c - k, c + k

        @pl.when(below >= 0)
        def _():
            z_up(below, n).wait_recv()

            @pl.when(c + 1 < nc)
            def _():
                z_up(below, n).start()

            if not split:
                others(lambda peer: x_out(below, peer).start())
            y_out(slab(below, d), n).start()

        @pl.when(above < nc)
        def _():
            z_dn(above, n).wait_recv()

            @pl.when(c > 0)
            def _():
                z_dn(above, n).start()

            if not split:
                others(lambda peer: x_out(above, peer).start())
            y_out(slab(above, d), n).start()

    def x_step(k):
        if split:
            return
        for s, valid in ([(c, c >= 0)] if k == 0 else [(c - k, c - k >= 0), (c + k, c + k < nc)]):
            @pl.when(valid)
            def _(s=s):
                def one(peer):
                    x_in(s, peer).wait_recv()
                    y_out(slab(s, peer), 0).start()
                others(one)

    groups_of_pairs = channels // 128
    chain(0)
    lax.fori_loop(0, groups_of_pairs // 2, diag, 0)
    for n in range(pieces):
        z_step(1, n)
    x_step(0)
    chain(1)
    lax.fori_loop(groups_of_pairs // 2, groups_of_pairs, diag, 0)
    for q in range(2, chunks):
        chain(q)
        if split and q == 2:
            for n in range(pieces):
                z_step(2, n)

    square[...] = jnp.zeros_like(square)

    def n_ref(head, q):
        return normed.at[head * chunks // (2 if split else 1) + q]

    def n_copy(q):
        return copy(n_ref(h, q), n_ref(h, q), n_send.at[q], n_recv.at[q], {"head": 1 - h})

    def n_in(q):
        return copy(n_ref(1 - h, q), n_ref(1 - h, q), n_send.at[q], n_recv.at[q], {"head": 1 - h})

    def r_copy(i):
        return copy(stage.at[i], normed.at[nc + h * (chunks // 2) + i], r_send.at[i], r_recv.at[i], {"dp": 1 - d})

    def f_ref(head, i):
        return normed.at[nc + head * (chunks // 2) + i]

    def f_copy(i):
        return copy(f_ref(h, i), f_ref(h, i), f_send.at[i], f_recv.at[i], {"head": 1 - h})

    def f_in(i):
        return copy(f_ref(1 - h, i), f_ref(1 - h, i), f_send.at[i], f_recv.at[i], {"head": 1 - h})

    def p_copy(n):
        return copy(p_out.at[n], p_in.at[n], p_send.at[n], p_recv.at[n], {"dp": 1 - d})

    def gated(q, put):
        for p in range(pairs):
            j = q * pairs + p
            lanes = lanes_of(j)
            piece = slice(p * 128, p * 128 + 128)
            carried = dot(c_map[...], held[q, :, piece])
            grown = jnp.exp(jnp.where(low, col[2 * j], col[2 * j + 1]))
            v = (y_ref[:, lanes] + carried * grown) * silu(gate[:, lanes].astype(F32))
            square[...] += v * v
            put(piece, (v * gain[:, lanes]).astype(BF16))

    if split:
        for i in range(chunks // 2):
            def put(piece, value, i=i):
                stage[i, :, piece] = value
            gated(2 * i + 1 - d, put)
            r_copy(i).start()
        for i in range(chunks // 2):
            def put(piece, value, i=i):
                normed[h * (chunks // 2) + i, :, piece] = value
            gated(2 * i + d, put)
            n_copy(i).start()
    else:
        for q in range(chunks):
            def put(piece, value, q=q):
                normed[h * chunks + q, :, piece] = value
            gated(q, put)
            n_copy(q).start()

    exchanged = chunks // 2 if split else chunks

    def q_copy():
        return copy(square, square_peer, q_sem.at[0], q_sem.at[1], {"head": 1 - h})

    q_copy().start()

    def project_full():
        width = 256

        def project(m, _):
            at = pl.ds(pl.multiple_of(m * width, width), width)
            acc = jnp.zeros((tok, width), F32)
            for q in range(2 * chunks):
                acc = acc + dot(normed[q], wfull[0, q * CHUNK : (q + 1) * CHUNK, at])
            out[:, at] = (acc * scale()).astype(BF16)
            return 0

        lax.fori_loop(0, features // width, project, 0)

    def scale():
        sums = jnp.sum(square[...] + square_peer[...], axis=1, keepdims=True)
        return lax.rsqrt(sums / (2 * channels) + 1e-05)

    def arrived(n):
        def one(b, _):
            @pl.when(b != own)
            def _():
                y_in(b, n).wait_recv()
            return 0
        lax.fori_loop(0, slabs, one, 0)

    if split:
        for i in range(chunks // 2):
            r_copy(i).wait_recv()
            f_copy(i).start()
        for k in range(3, nc):
            for n in range(pieces):
                z_step(k, n)
        for i in range(chunks // 2):
            f_in(i).wait_recv()
            n_in(i).wait_recv()
        q_copy().wait_recv()
        width = 256
        tiles = piece_width // width
        for n in range(pieces):
            arrived(n)
            for t in range(tiles):
                at = slice(t * width, t * width + width)
                acc = jnp.zeros((tok, width), F32)
                for cc in range(nc):
                    acc = acc + dot(normed[nc + cc], wfull[n, cc * rows : (cc + 1) * rows, at])
                p_out[n, :, at] = acc.astype(BF16)
            p_copy(n).start()
            for t in range(tiles):
                at = slice(t * width, t * width + width)
                acc = jnp.zeros((tok, width), F32)
                for cc in range(nc):
                    acc = acc + dot(normed[cc], wfull[n, cc * rows : (cc + 1) * rows, at])
                acc_ref[n, :, at] = acc
        for n in range(pieces):
            p_copy(n).wait_recv()
            out[:, n * piece_width : (n + 1) * piece_width] = (
                (acc_ref[n] + p_in[n].astype(F32)) * scale()
            ).astype(BF16)
        for i in range(chunks // 2):
            r_copy(i).wait_send()
            f_copy(i).wait_send()
        for n in range(pieces):
            p_copy(n).wait_send()
    else:
        for k in range(2, nc):
            z_step(k, 0)
            x_step(k - 1)
        x_step(nc - 1)
        for q in range(chunks):
            n_in(q).wait_recv()
        q_copy().wait_recv()
        arrived(0)
        project_full()

    if not split:
        def sent_x(s, _):
            others(lambda peer: x_out(s, peer).wait_send())
            return 0

        lax.fori_loop(0, nc, sent_x, 0)

    def sent_y(b, _):
        @pl.when(b != own)
        def _():
            for n in range(pieces):
                y_out(b, n).wait_send()
        return 0

    lax.fori_loop(0, slabs, sent_y, 0)

    @pl.when(c + 1 < nc)
    def _():
        for one in edges():
            one.wait_send()
        for q in range(chunks):
            st_copy(q).wait_send()

        def sent(s, _):
            for n in range(pieces):
                z_up(s, n).wait_send()
            return 0
        lax.fori_loop(0, c + 1, sent, 0)

    @pl.when(c > 0)
    def _():
        def sent(s, _):
            for n in range(pieces):
                z_dn(s, n).wait_send()
            return 0
        lax.fori_loop(c, nc, sent, 0)

    for q in range(exchanged):
        n_copy(q).wait_send()
    q_copy().wait_send()


def on_device(sizes, ssm, maps, gate, step_raw, taps, bias, map_taps, map_bias, step_bias, decay, skip, gain, w):
    nc, nd, ng = sizes
    tok, channels = ssm.shape[1:]
    heads = step_raw.shape[2]
    n_state = maps.shape[2] // 2
    features = w.shape[1]
    chunks = channels // CHUNK
    split = nd == 2 and w.shape[0] == CHUNK and nc == 2 * chunks // 2
    slabs = nc if split else nc * nd
    pieces = PIECES if split else 1
    width = features // pieces
    dma = pltpu.SemaphoreType.DMA
    vmem = pl.BlockSpec(memory_space=pltpu.VMEM)
    operands = (
        ssm[0], maps[0], gate[0], jnp.swapaxes(step_raw[0], 0, 1), taps, bias[None], map_taps, map_bias[None],
        step_bias[None], decay[None], skip[None], gain[None], w,
    )
    result = pl.pallas_call(
        functools.partial(kernel, sizes, split),
        out_shape=jax.ShapeDtypeStruct((tok, features), BF16),
        in_specs=[pl.BlockSpec(memory_space=pltpu.HBM)] * len(operands),
        out_specs=vmem,
        scratch_shapes=[pltpu.VMEM(a.shape, a.dtype) for a in operands[:-1]] + [
            pltpu.VMEM((pieces, slabs * w.shape[0], width), BF16),
            pltpu.VMEM((2 * chunks, tok, CHUNK), BF16),
            pltpu.VMEM((n_state, channels), F32),
            pltpu.VMEM((chunks, n_state, CHUNK), BF16),
            pltpu.VMEM((chunks, n_state, CHUNK), BF16),
            pltpu.VMEM((tok, channels), F32),
            pltpu.VMEM((tok, channels), BF16),
            pltpu.VMEM((heads, tok, 128), F32),
            pltpu.VMEM((heads, tok), F32),
            pltpu.VMEM((heads, tok), F32),
            pltpu.VMEM((heads, tok), F32),
            pltpu.VMEM((tok, tok), F32),
            pltpu.VMEM((n_state, tok), F32),
            pltpu.VMEM((tok, n_state), BF16),
            pltpu.VMEM((EDGE, channels), BF16),
            pltpu.VMEM((EDGE, 2 * n_state), BF16),
            pltpu.VMEM((tok + 8, 128), F32),
            pltpu.VMEM((tok + 8, 2 * n_state), F32),
            pltpu.VMEM((tok + tok // 2, 128), F32),
            pltpu.VMEM((tok, 128), F32),
            pltpu.VMEM((tok, 128), F32),
            pltpu.VMEM((heads, 8, 128), F32),
            pltpu.VMEM((chunks // 2, tok, CHUNK), BF16),
            pltpu.VMEM((pieces, tok, width), F32),
            pltpu.VMEM((pieces, tok, width), BF16),
            pltpu.VMEM((pieces, tok, width), BF16),
            dma((len(operands),)), dma((pieces,)), dma((2,)), dma((2,)),
            dma((pieces * nc,)), dma((pieces * nc,)), dma((pieces * nc,)),
            dma((nc * nd,)), dma((nc * nd,)), dma((pieces * slabs,)), dma((pieces * slabs,)),
            dma((chunks,)), dma((chunks,)), dma((chunks,)), dma((chunks,)), dma((2,)),
            dma((chunks,)), dma((chunks,)), dma((chunks,)), dma((chunks,)), dma((pieces,)), dma((pieces,)),
        ],
        compiler_params=pltpu.CompilerParams(
            collective_id=0, has_side_effects=True, vmem_limit_bytes=48 * 1024 * 1024
        ),
    )(*operands)
    return result[None]


def solution(mesh):
    sizes = (mesh.shape["ctx"], mesh.shape["dp"], mesh.shape["groups"])
    placed = (
        P(("groups", "dp"), "ctx", "head"),
        P(("groups", "dp"), "ctx", None),
        P(("groups", "dp"), "ctx", "head"),
        P(("groups", "dp"), "ctx", "head"),
        P(None, "head"),
        P("head"),
        P(),
        P(),
        P("head"),
        P("head"),
        P("head"),
        P("head"),
        P(("ctx", "dp"), "head"),
    )
    return jax.shard_map(
        functools.partial(on_device, sizes),
        mesh=mesh,
        in_specs=placed,
        out_specs=P(("groups", "dp"), "ctx", "head"),
        check_vma=False,
    )
```

```python
import functools

import jax
import jax.numpy as jnp
from jax import lax
from jax.experimental import pallas as pl
from jax.experimental.pallas import tpu as pltpu
from jax.sharding import PartitionSpec as P

MESH = pl.DeviceIdType.MESH
F32, BF16 = jnp.float32, jnp.bfloat16
EDGE = 16
CHUNK = 512
PIECES = 4


def silu(v):
    return 0.5 * v * (1.0 + jnp.tanh(0.5 * v))


def dot(a, b):
    return jnp.dot(a, b, preferred_element_type=F32)


def kernel(
    sizes, split,
    *refs,
):
    n_in_refs = 13
    hbm = refs[:n_in_refs]
    out = refs[n_in_refs]
    local = refs[n_in_refs + 1 : 2 * n_in_refs]
    (
        wfull, normed, states, held, handed, y_ref, xs_ref, col, cum_t, tail_t, step_t, scores, b_t, c_map,
        edge_x, edge_m, pad, pad_m, cum_buf, square, square_peer, skip_col, stage, acc_ref, p_out, p_in,
        in_sem, w_sem, edge_send, edge_recv, zup_sem, zdn_sem, z_recv, x_send, x_recv, y_send, y_recv,
        st_send, st_recv, n_send, n_recv, q_sem, r_send, r_recv, f_send, f_recv, p_send, p_recv,
    ) = refs[2 * n_in_refs :]
    w_in = hbm[-1]
    ssm, maps, gate, step_raw, taps, bias, map_taps, map_bias, step_bias, decay, skip, gain = local
    nc, nd, ng = sizes
    tok, channels = ssm.shape
    heads = step_raw.shape[0]
    rows = w_in.shape[0]
    features = w_in.shape[1]
    pieces, piece_width, _ = wfull.shape[0], wfull.shape[2], 0
    part = rows // 2 if split else max(16, (rows * 3 // 8) // 16 * 16)
    mine = rows - part
    chunks = channels // CHUNK
    pairs = CHUNK // 128
    g, c = lax.axis_index("groups"), lax.axis_index("ctx")
    d, h = lax.axis_index("dp"), lax.axis_index("head")
    half = tok // 2

    def span(start, size):
        return pl.ds(pl.multiple_of(start, 16), size)

    def slab(cc, dd):
        return cc if split else cc * nd + dd

    slabs = nc if split else nc * nd

    def mine_of(cc, dd, n):
        return wfull.at[n, span(slab(cc, dd) * rows + g * part, mine)]

    def copy(src, dst, send, recv, target):
        return pltpu.make_async_remote_copy(
            src_ref=src, dst_ref=dst, send_sem=send, recv_sem=recv,
            device_id=target, device_id_type=MESH,
        )

    def z_up(s, n):
        ref, at = mine_of(s, d, n), n * nc + s
        return copy(ref, ref, zup_sem.at[at], z_recv.at[at], {"ctx": c + 1})

    def z_dn(s, n):
        ref, at = mine_of(s, d, n), n * nc + s
        return copy(ref, ref, zdn_sem.at[at], z_recv.at[at], {"ctx": c - 1})

    def x_out(s, peer):
        ref = mine_of(s, d, 0)
        return copy(ref, ref, x_send.at[slab(s, peer)], x_recv.at[slab(s, d)], {"dp": peer})

    def x_in(s, peer):
        ref = mine_of(s, peer, 0)
        return copy(ref, ref, x_send.at[slab(s, peer)], x_recv.at[slab(s, peer)], {"dp": peer})

    def y_out(b, n):
        ref, at = wfull.at[n, span(b * rows + g * mine, part)], n * slabs + b
        return copy(ref, ref, y_send.at[at], y_recv.at[at], {"groups": 1 - g})

    def y_in(b, n):
        ref, at = wfull.at[n, span(b * rows + (1 - g) * mine, part)], n * slabs + b
        return copy(ref, ref, y_send.at[at], y_recv.at[at], {"groups": 1 - g})

    def others(do):
        def one(o, _):
            do(lax.rem(d + o, nd))
            return 0
        lax.fori_loop(1, nd, one, 0)

    own = slab(c, d)
    loads = [
        pltpu.make_async_copy(
            w_in.at[:, n * piece_width : (n + 1) * piece_width], wfull.at[n, span(own * rows, rows)], w_sem.at[n]
        )
        for n in range(pieces)
    ]
    fetches = [pltpu.make_async_copy(a, b, in_sem.at[i]) for i, (a, b) in enumerate(zip(hbm[:-1], local))]
    for one in loads + fetches:
        one.start()

    barrier = pltpu.get_barrier_semaphore()

    def greet(target):
        pl.semaphore_signal(barrier, inc=1, device_id=target, device_id_type=MESH)

    @pl.when(c > 0)
    def _():
        greet({"ctx": c - 1})

    @pl.when(c + 1 < nc)
    def _():
        greet({"ctx": c + 1})

    others(lambda peer: greet({"dp": peer}))
    greet({"groups": 1 - g})
    greet({"head": 1 - h})
    for one in loads + fetches[:2]:
        one.wait()
    pl.semaphore_wait(barrier, nd + 1 + jnp.where(c > 0, 1, 0) + jnp.where(c + 1 < nc, 1, 0))

    def edges():
        return (
            copy(ssm.at[pl.ds(tok - EDGE, EDGE)], edge_x, edge_send.at[0], edge_recv.at[0], {"ctx": c + 1}),
            copy(maps.at[pl.ds(tok - EDGE, EDGE)], edge_m, edge_send.at[1], edge_recv.at[1], {"ctx": c + 1}),
        )

    @pl.when(c + 1 < nc)
    def _():
        for one in edges():
            one.start()
        for n in range(pieces):
            z_up(c, n).start()

    @pl.when(c > 0)
    def _():
        for n in range(pieces):
            z_dn(c, n).start()

    if not split:
        others(lambda peer: x_out(c, peer).start())

    for one in fetches[2:]:
        one.wait()

    cum_buf[...] = jnp.zeros_like(cum_buf)
    cum_buf[:heads, :] = step_raw[:, :half]
    cum_buf[half : half + heads, :] = step_raw[:, half:]
    raw_top = jnp.transpose(cum_buf[:half, :])
    raw_bottom = jnp.transpose(cum_buf[half : tok, :])
    raw = jnp.concatenate([raw_top, raw_bottom], axis=0)[:, :heads] + step_bias[...]
    step = jnp.maximum(raw, 0.0) + jnp.log1p(jnp.exp(-jnp.abs(raw)))
    cum_buf[...] = jnp.zeros_like(cum_buf)
    cum_buf[half : half + tok, :heads] = step
    step_t[...] = jnp.transpose(cum_buf[half : half + tok, :])[: step_t.shape[0]]
    cum_buf[half : half + tok, :heads] = step * -jnp.exp(decay[...])
    by = 1
    while by < tok:
        cum_buf[half : half + tok, :] = cum_buf[half : half + tok, :] + cum_buf[half - by : half - by + tok, :]
        by *= 2
    cum = cum_buf[half : half + tok, :]
    cum_t[...] = jnp.transpose(cum)[: cum_t.shape[0]]
    tail_t[...] = jnp.exp(cum_t[:, tok - 1 : tok] - cum_t[...]) * step_t[...]
    for i in range(heads):
        col[i] = jnp.broadcast_to(cum[:, i : i + 1], (tok, 128))
        skip_col[i] = jnp.broadcast_to(skip[:, i : i + 1], (8, 128))

    @pl.when(c == 0)
    def _():
        edge_x[...] = jnp.zeros_like(edge_x)
        edge_m[...] = jnp.zeros_like(edge_m)
        held[...] = jnp.zeros_like(held)

    @pl.when(c > 0)
    def _():
        for one in edges():
            one.wait_recv()

    low = lax.broadcasted_iota(jnp.int32, (1, 128), 1) < channels // heads

    pad_m[0:8] = edge_m[...].astype(F32)[EDGE - 8 :]
    pad_m[8 : 8 + tok] = maps[...].astype(F32)
    total = jnp.broadcast_to(map_bias[...], (tok, maps.shape[1]))
    for k in range(4):
        total = total + map_taps[k : k + 1, :] * pad_m[5 + k : 5 + k + tok]
    both = silu(total).astype(BF16)
    n_state = maps.shape[1] // 2
    c_map[...] = both[:, n_state:]
    b_t[...] = jnp.transpose(both[:, :n_state].astype(F32))
    scores[...] = dot(c_map[...], b_t[...].astype(BF16))

    def lanes_of(j):
        return pl.ds(pl.multiple_of(j * 128, 128), 128)

    def first(j, _):
        lanes = lanes_of(j)
        pad[0:8] = edge_x[:, lanes].astype(F32)[EDGE - 8 :]
        pad[8 : 8 + tok] = ssm[:, lanes].astype(F32)
        total = jnp.broadcast_to(bias[:, lanes], (tok, 128))
        for k in range(4):
            total = total + taps[k : k + 1, lanes] * pad[5 + k : 5 + k + tok]
        xs = silu(total).astype(BF16)
        xs_ref[:, lanes] = xs
        parts = []
        for i in range(2):
            weighted = (b_t[...] * tail_t[pl.ds(2 * j + i, 1), :]).astype(BF16)
            parts.append(dot(weighted, xs))
        states[:, lanes] = jnp.where(low, parts[0], parts[1])
        return 0

    lax.fori_loop(0, channels // 128, first, 0)

    def st_copy(q):
        return copy(handed.at[q], held.at[q], st_send.at[q], st_recv.at[q], {"ctx": c + 1})

    def chain(q):
        @pl.when(c > 0)
        def _():
            st_copy(q).wait_recv()

        @pl.when(c + 1 < nc)
        def _():
            for p in range(pairs):
                j = q * pairs + p
                decayed = jnp.where(low, col[2 * j, tok - 1 : tok, :], col[2 * j + 1, tok - 1 : tok, :])
                piece = slice(p * 128, p * 128 + 128)
                following = jnp.exp(decayed) * held[q, :, piece].astype(F32) + states[:, j * 128 : j * 128 + 128]
                handed[q, :, piece] = following.astype(BF16)
            st_copy(q).start()

    rows_i = lax.broadcasted_iota(jnp.int32, (half, half), 0)
    cols_i = lax.broadcasted_iota(jnp.int32, (half, half), 1)
    causal = rows_i >= cols_i

    def diag(j, _):
        lanes = lanes_of(j)
        xs = xs_ref[:, lanes]
        tops, bottoms = [], []
        for i in range(2):
            at = 2 * j + i
            row = cum_t[pl.ds(at, 1), :]
            sized = step_t[pl.ds(at, 1), :]
            column = col[at]
            upper, lower = column[:half], column[half:]
            q00 = scores[:half, :half] * jnp.exp(jnp.where(causal, upper - row[:, :half], -jnp.inf)) * sized[:, :half]
            q10 = scores[half:, :half] * jnp.exp(lower - row[:, :half]) * sized[:, :half]
            q11 = scores[half:, half:] * jnp.exp(jnp.where(causal, lower - row[:, half:], -jnp.inf)) * sized[:, half:]
            tops.append(dot(q00.astype(BF16), xs[:half]))
            bottoms.append(dot(q10.astype(BF16), xs[:half]) + dot(q11.astype(BF16), xs[half:]))
        skips = jnp.where(low, skip_col[2 * j, 0:1, :], skip_col[2 * j + 1, 0:1, :])
        y_ref[:half, lanes] = jnp.where(low, tops[0], tops[1]) + skips * xs[:half].astype(F32)
        y_ref[half:, lanes] = jnp.where(low, bottoms[0], bottoms[1]) + skips * xs[half:].astype(F32)
        return 0

    def z_step(k, n):
        z_from_below(k, n)
        z_from_above(k, n)

    def z_from_below(k, n):
        below = c - k

        @pl.when(below >= 0)
        def _():
            z_up(below, n).wait_recv()

            @pl.when(c + 1 < nc)
            def _():
                z_up(below, n).start()

            if not split:
                others(lambda peer: x_out(below, peer).start())
            y_out(slab(below, d), n).start()

    def z_from_above(k, n):
        above = c + k

        @pl.when(above < nc)
        def _():
            z_dn(above, n).wait_recv()

            @pl.when(c > 0)
            def _():
                z_dn(above, n).start()

            if not split:
                others(lambda peer: x_out(above, peer).start())
            y_out(slab(above, d), n).start()

    def x_step(k):
        if split:
            return
        for s, valid in ([(c, c >= 0)] if k == 0 else [(c - k, c - k >= 0), (c + k, c + k < nc)]):
            @pl.when(valid)
            def _(s=s):
                def one(peer):
                    x_in(s, peer).wait_recv()
                    y_out(slab(s, peer), 0).start()
                others(one)

    square[...] = jnp.zeros_like(square)

    def n_ref(head, q):
        return normed.at[head * chunks // (2 if split else 1) + q]

    def n_copy(q):
        return copy(n_ref(h, q), n_ref(h, q), n_send.at[q], n_recv.at[q], {"head": 1 - h})

    def n_in(q):
        return copy(n_ref(1 - h, q), n_ref(1 - h, q), n_send.at[q], n_recv.at[q], {"head": 1 - h})

    def r_copy(i):
        return copy(stage.at[2 * i + 1 - d], normed.at[nc + h * (chunks // 2) + i], r_send.at[i], r_recv.at[i], {"dp": 1 - d})

    def f_ref(head, i):
        return normed.at[nc + head * (chunks // 2) + i]

    def f_copy(i):
        return copy(f_ref(h, i), f_ref(h, i), f_send.at[i], f_recv.at[i], {"head": 1 - h})

    def f_in(i):
        return copy(f_ref(1 - h, i), f_ref(1 - h, i), f_send.at[i], f_recv.at[i], {"head": 1 - h})

    def p_copy(n):
        return copy(p_out.at[n], p_in.at[n], p_send.at[n], p_recv.at[n], {"dp": 1 - d})

    def gated(q, put):
        for p in range(pairs):
            j = q * pairs + p
            lanes = lanes_of(j)
            piece = slice(p * 128, p * 128 + 128)
            carried = dot(c_map[...], held[q, :, piece])
            grown = jnp.exp(jnp.where(low, col[2 * j], col[2 * j + 1]))
            v = (y_ref[:, lanes] + carried * grown) * silu(gate[:, lanes].astype(F32))
            square[...] += v * v
            put(piece, (v * gain[:, lanes]).astype(BF16))

    def gate_chunk(q):
        def put(piece, value):
            stage[q, :, piece] = value
        gated(q, put)
        if split:
            @pl.when(d != q % 2)
            def _():
                r_copy(q // 2).start()

            @pl.when(d == q % 2)
            def _():
                normed[h * (chunks // 2) + q // 2] = stage[q]
                n_copy(q // 2).start()
        else:
            normed[h * chunks + q] = stage[q]
            n_copy(q).start()

    def diag_chunk(q):
        lax.fori_loop(q * pairs, (q + 1) * pairs, diag, 0)

    for q in range(chunks):
        chain(q)
        if q > 0:
            gate_chunk(q - 1)
        diag_chunk(q)
        if q == 1:
            for n in range(pieces):
                z_from_above(1, n)
    for n in range(pieces):
        z_from_below(1, n)
    gate_chunk(chunks - 1)
    x_step(0)

    exchanged = chunks // 2 if split else chunks

    def q_copy():
        return copy(square, square_peer, q_sem.at[0], q_sem.at[1], {"head": 1 - h})

    q_copy().start()

    def project_full():
        width = 256

        def project(m, _):
            at = pl.ds(pl.multiple_of(m * width, width), width)
            acc = jnp.zeros((tok, width), F32)
            for q in range(2 * chunks):
                acc = acc + dot(normed[q], wfull[0, q * CHUNK : (q + 1) * CHUNK, at])
            out[:, at] = (acc * scale()).astype(BF16)
            return 0

        lax.fori_loop(0, features // width, project, 0)

    def scale():
        sums = jnp.sum(square[...] + square_peer[...], axis=1, keepdims=True)
        return lax.rsqrt(sums / (2 * channels) + 1e-05)

    def arrived(n):
        def one(b, _):
            @pl.when(b != own)
            def _():
                y_in(b, n).wait_recv()
            return 0
        lax.fori_loop(0, slabs, one, 0)

    if split:
        for n in range(pieces):
            z_step(2, n)
        for i in range(chunks // 2):
            r_copy(i).wait_recv()
            f_copy(i).start()
        for k in range(3, nc):
            for n in range(pieces):
                z_step(k, n)
        for i in range(chunks // 2):
            f_in(i).wait_recv()
            n_in(i).wait_recv()
        q_copy().wait_recv()
        width = 256
        tiles = piece_width // width
        for n in range(pieces):
            arrived(n)
            for t in range(tiles):
                at = slice(t * width, t * width + width)
                acc = jnp.zeros((tok, width), F32)
                for cc in range(nc):
                    acc = acc + dot(normed[nc + cc], wfull[n, cc * rows : (cc + 1) * rows, at])
                p_out[n, :, at] = acc.astype(BF16)
            p_copy(n).start()
            for t in range(tiles):
                at = slice(t * width, t * width + width)
                acc = jnp.zeros((tok, width), F32)
                for cc in range(nc):
                    acc = acc + dot(normed[cc], wfull[n, cc * rows : (cc + 1) * rows, at])
                acc_ref[n, :, at] = acc
        for n in range(pieces):
            p_copy(n).wait_recv()
            out[:, n * piece_width : (n + 1) * piece_width] = (
                (acc_ref[n] + p_in[n].astype(F32)) * scale()
            ).astype(BF16)
        for i in range(chunks // 2):
            r_copy(i).wait_send()
            f_copy(i).wait_send()
        for n in range(pieces):
            p_copy(n).wait_send()
    else:
        for k in range(2, nc):
            z_step(k, 0)
            x_step(k - 1)
        x_step(nc - 1)
        for q in range(chunks):
            n_in(q).wait_recv()
        q_copy().wait_recv()
        arrived(0)
        project_full()

    if not split:
        def sent_x(s, _):
            others(lambda peer: x_out(s, peer).wait_send())
            return 0

        lax.fori_loop(0, nc, sent_x, 0)

    def sent_y(b, _):
        @pl.when(b != own)
        def _():
            for n in range(pieces):
                y_out(b, n).wait_send()
        return 0

    lax.fori_loop(0, slabs, sent_y, 0)

    @pl.when(c + 1 < nc)
    def _():
        for one in edges():
            one.wait_send()
        for q in range(chunks):
            st_copy(q).wait_send()

        def sent(s, _):
            for n in range(pieces):
                z_up(s, n).wait_send()
            return 0
        lax.fori_loop(0, c + 1, sent, 0)

    @pl.when(c > 0)
    def _():
        def sent(s, _):
            for n in range(pieces):
                z_dn(s, n).wait_send()
            return 0
        lax.fori_loop(c, nc, sent, 0)

    for q in range(exchanged):
        n_copy(q).wait_send()
    q_copy().wait_send()


def on_device(sizes, ssm, maps, gate, step_raw, taps, bias, map_taps, map_bias, step_bias, decay, skip, gain, w):
    nc, nd, ng = sizes
    tok, channels = ssm.shape[1:]
    heads = step_raw.shape[2]
    n_state = maps.shape[2] // 2
    features = w.shape[1]
    chunks = channels // CHUNK
    split = nd == 2 and w.shape[0] == CHUNK and nc == 2 * chunks // 2
    slabs = nc if split else nc * nd
    pieces = PIECES if split else 1
    width = features // pieces
    dma = pltpu.SemaphoreType.DMA
    vmem = pl.BlockSpec(memory_space=pltpu.VMEM)
    operands = (
        ssm[0], maps[0], gate[0], jnp.swapaxes(step_raw[0], 0, 1), taps, bias[None], map_taps, map_bias[None],
        step_bias[None], decay[None], skip[None], gain[None], w,
    )
    result = pl.pallas_call(
        functools.partial(kernel, sizes, split),
        out_shape=jax.ShapeDtypeStruct((tok, features), BF16),
        in_specs=[pl.BlockSpec(memory_space=pltpu.HBM)] * len(operands),
        out_specs=vmem,
        scratch_shapes=[pltpu.VMEM(a.shape, a.dtype) for a in operands[:-1]] + [
            pltpu.VMEM((pieces, slabs * w.shape[0], width), BF16),
            pltpu.VMEM((2 * chunks, tok, CHUNK), BF16),
            pltpu.VMEM((n_state, channels), F32),
            pltpu.VMEM((chunks, n_state, CHUNK), BF16),
            pltpu.VMEM((chunks, n_state, CHUNK), BF16),
            pltpu.VMEM((tok, channels), F32),
            pltpu.VMEM((tok, channels), BF16),
            pltpu.VMEM((heads, tok, 128), F32),
            pltpu.VMEM((heads, tok), F32),
            pltpu.VMEM((heads, tok), F32),
            pltpu.VMEM((heads, tok), F32),
            pltpu.VMEM((tok, tok), F32),
            pltpu.VMEM((n_state, tok), F32),
            pltpu.VMEM((tok, n_state), BF16),
            pltpu.VMEM((EDGE, channels), BF16),
            pltpu.VMEM((EDGE, 2 * n_state), BF16),
            pltpu.VMEM((tok + 8, 128), F32),
            pltpu.VMEM((tok + 8, 2 * n_state), F32),
            pltpu.VMEM((tok + tok // 2, 128), F32),
            pltpu.VMEM((tok, 128), F32),
            pltpu.VMEM((tok, 128), F32),
            pltpu.VMEM((heads, 8, 128), F32),
            pltpu.VMEM((chunks, tok, CHUNK), BF16),
            pltpu.VMEM((pieces, tok, width), F32),
            pltpu.VMEM((pieces, tok, width), BF16),
            pltpu.VMEM((pieces, tok, width), BF16),
            dma((len(operands),)), dma((pieces,)), dma((2,)), dma((2,)),
            dma((pieces * nc,)), dma((pieces * nc,)), dma((pieces * nc,)),
            dma((nc * nd,)), dma((nc * nd,)), dma((pieces * slabs,)), dma((pieces * slabs,)),
            dma((chunks,)), dma((chunks,)), dma((chunks,)), dma((chunks,)), dma((2,)),
            dma((chunks,)), dma((chunks,)), dma((chunks,)), dma((chunks,)), dma((pieces,)), dma((pieces,)),
        ],
        compiler_params=pltpu.CompilerParams(
            collective_id=0, has_side_effects=True, vmem_limit_bytes=63 * 1024 * 1024
        ),
    )(*operands)
    return result[None]


def solution(mesh):
    sizes = (mesh.shape["ctx"], mesh.shape["dp"], mesh.shape["groups"])
    placed = (
        P(("groups", "dp"), "ctx", "head"),
        P(("groups", "dp"), "ctx", None),
        P(("groups", "dp"), "ctx", "head"),
        P(("groups", "dp"), "ctx", "head"),
        P(None, "head"),
        P("head"),
        P(),
        P(),
        P("head"),
        P("head"),
        P("head"),
        P("head"),
        P(("ctx", "dp"), "head"),
    )
    return jax.shard_map(
        functools.partial(on_device, sizes),
        mesh=mesh,
        in_specs=placed,
        out_specs=P(("groups", "dp"), "ctx", "head"),
        check_vma=False,
    )
```
